32 devices in a mesh: frag: 1, alpha: 8 (over z, y), beta: 2 (over x), orb: 2 (over core).
Axes of the slice: x: 2, y: 2, z: 4, core: 2. Of those that a mesh axis runs over, the one named last changes fastest.
Arguments:
- civec: bfloat16 [2048, 8192], P(('frag', 'alpha'), ('beta', 'orb')), may hold values from -1 to 1
- alpha_coupling: bfloat16 [96, 128, 128], P('frag'), may hold values from -0.5 to 0.5
- alpha_source: int32 [96], P('frag'), may hold values from 0 to 15
- alpha_pair: int32 [96], P('frag'), may hold values from 0 to 783
- alpha_count: int32 [16], P('frag'), may hold values from 1 to 6, 64 in all
- beta_coupling: bfloat16 [1024, 128, 128], P(('frag', 'beta', 'orb')), may hold values from -0.5 to 0.5
- beta_source: int32 [1024], P(('frag', 'beta', 'orb')), may hold values from 0 to 63
- beta_pair: int32 [1024], P(('frag', 'beta', 'orb')), may hold values from 0 to 783
- beta_count: int32 [64], P(('frag', 'beta', 'orb')), may hold values from 1 to 16, 682 in all
Outputs:
- gamma: float32 [2, 784, 784], P('frag', 'alpha', ('beta', 'orb'))
The draws below stay inside these ranges and needn't reach their ends.
All inputs are finite; a program needn't handle non-finite values. No bound on the sum of `beta_count` on one device may be relied on, other than what follows from the above.
Results may differ from the reference program's by a relative error of at most 0.0003.
Values may be sent and summed in bfloat16 or wider, within the bound.
A program may use at most 192 MiB of HBM per device.

```python
import math
import jax
import jax.numpy as jnp
import numpy as np
from jax import lax

TILE = 128
CAPA = 6
CAPB = 16
NPAIR = 784
NA = 16
NB = 64


def draw_civec(key, part):
    key = jax.random.fold_in(key, 11)
    key_noise, key_rows, key_cols = jax.random.split(key, 3)
    height = NA * TILE
    breadth = NB * TILE
    factor = 1.0 / (TILE * math.sqrt(NB) * 21.5)
    col_scale = jnp.exp(jax.random.uniform(key_cols, (1, breadth), jnp.float32, 0.0, math.log(10.0)))
    noise = jax.random.truncated_normal(key_noise, -4.0, 4.0, (height, breadth), jnp.float32)
    row_scale = jnp.exp(jax.random.uniform(key_rows, (height, 1), jnp.float32, 0.0, math.log(10.0)))
    return (noise * row_scale * col_scale * factor).astype(jnp.bfloat16)


def set_ends(drawn, rng, low, top_value):
    spot = [jax.random.randint(jax.random.fold_in(rng, axis), (), 0, length) for axis, length in enumerate(drawn.shape)]
    longest = drawn.shape.index(max(drawn.shape))
    next_to = spot[:longest] + [(spot[longest] + 1) % drawn.shape[longest]] + spot[longest + 1:]
    return drawn.at[tuple(spot)].set(low).at[tuple(next_to)].set(top_value)


def block_levels(rng, shape, cuts, least, largest):
    def one(dim, blocks):
        draws = jax.random.uniform(jax.random.fold_in(jax.random.fold_in(rng, 6), dim), (blocks,), jnp.float32, least / len(cuts), largest / len(cuts))
        return jnp.repeat(jnp.exp(draws), shape[dim] // blocks).reshape((-1,) + (1,) * (len(shape) - dim - 1))

    loudness = one(*cuts[0])
    for cut in cuts[1:]:
        loudness = loudness * one(*cut)
    return loudness


def length_profile(number_of, total, limit, lean):
    weights = [(1 << 20) // math.isqrt(grade ** lean) + 1 for grade in range(2, number_of + 1)]
    rest, given = total - limit - (number_of - 1), [1] * (number_of - 1)
    while rest > 0:
        candidates = [i for i in range(number_of - 1) if given[i] < limit]
        pool, budget = sum([weights[i] for i in candidates]), rest
        for i in candidates:
            more = min(limit - given[i], max(1, budget * weights[i] // pool), rest)
            given[i] = given[i] + more
            rest = rest - more
    return np.array([limit] + given)


def uneven(key, count, total, most, slope):
    if count == 2:
        one = jax.random.randint(key, (), max(1, total - most), min(most, total - 1) + 1)
        return jnp.stack([one, total - one])
    sizes = jnp.asarray(length_profile(count, total, most, slope), jnp.int32)
    twos = (count - 1) // 2
    source_of, sink = sizes[1:1 + 2 * twos:2], sizes[2:2 + 2 * twos:2]
    room = jnp.minimum(source_of - 1, most - sink)
    shifted = jax.random.randint(jax.random.fold_in(key, 1), (twos,), 0, 1 << 20) % (room + 1)
    sizes = sizes.at[1:1 + 2 * twos:2].set(source_of - shifted).at[2:2 + 2 * twos:2].set(sink + shifted)
    return sizes[jax.random.permutation(jax.random.fold_in(key, 2), count)]


def normal_values(key, extent, width, limit, cuts=(), held_as=jnp.bfloat16):
    drawn = jax.random.normal(key, extent, jnp.float32) * width
    if len(cuts) > 0:
        drawn = block_levels(key, extent, cuts, -0.22, 0.18) * drawn
    return jnp.clip(drawn, min=-limit, max=limit).astype(held_as)


def setup_inputs(seed: int = 0, part: int = 0) -> dict:
    key_list = jax.random.split(jax.random.key(seed), 10)
    part_splits = jax.random.split(jax.random.fold_in(key_list[9], part), 10)
    civec = draw_civec(jax.random.fold_in(jax.random.fold_in(key_list[9], part), 71), part)
    alpha_coupling = normal_values(part_splits[1], (NA * CAPA, TILE, TILE), TILE ** -0.5, 0.5)
    alpha_source = set_ends(jax.random.randint(part_splits[2], (NA * CAPA,), 0, NA), jax.random.fold_in(part_splits[2], 1), 0, NA - 1).astype(jnp.int32)
    alpha_pair = set_ends(jax.random.randint(part_splits[3], (NA * CAPA,), 0, NPAIR), jax.random.fold_in(part_splits[3], 1), 0, NPAIR - 1).astype(jnp.int32)
    alpha_count = uneven(part_splits[4], NA, NA * CAPA * 2 // 3, CAPA, 2).astype(jnp.int32)
    beta_coupling = normal_values(part_splits[5], (NB * CAPB, TILE, TILE), TILE ** -0.5, 0.5, ((0, 4),))
    beta_source = set_ends(jax.random.randint(part_splits[6], (NB * CAPB,), 0, NB), jax.random.fold_in(part_splits[6], 1), 0, NB - 1).astype(jnp.int32)
    beta_pair = set_ends(jax.random.randint(part_splits[7], (NB * CAPB,), 0, NPAIR), jax.random.fold_in(part_splits[7], 1), 0, NPAIR - 1).astype(jnp.int32)
    beta_count = uneven(part_splits[8], NB, NB * CAPB * 2 // 3, CAPB, 2).astype(jnp.int32)
    return {"civec": civec, "alpha_coupling": alpha_coupling, "alpha_source": alpha_source, "alpha_pair": alpha_pair, "alpha_count": alpha_count, "beta_coupling": beta_coupling, "beta_source": beta_source, "beta_pair": beta_pair, "beta_count": beta_count}


def pair_density(grams, pair_index):
    units, slots, _ = grams.shape
    onehot = (pair_index[:, None] == jnp.arange(NPAIR, dtype=jnp.int32)[None, :]).astype(jnp.float32)
    onehot = onehot.reshape(units, slots, NPAIR)
    weighted = jnp.einsum('ukl,ulq->ukq', grams, onehot, precision=lax.Precision.HIGHEST)
    return jnp.einsum('ukp,ukq->pq', onehot, weighted, precision=lax.Precision.HIGHEST)


def reference(civec, alpha_coupling, alpha_source, alpha_pair, alpha_count, beta_coupling, beta_source, beta_pair, beta_count):
    alpha_blocks = civec.reshape(NA, TILE, NB * TILE)

    def alpha_target(inputs):
        couplings, sources, filled = inputs
        picked = jnp.take(alpha_blocks, sources.astype(jnp.int32), axis=0).astype(jnp.float32)
        images = jnp.einsum('sij,sjw->siw', couplings.astype(jnp.float32), picked)
        occupied = (jnp.arange(CAPA, dtype=jnp.int32) < filled).astype(jnp.float32)
        images = (images * occupied[:, None, None]).astype(jnp.bfloat16).reshape(CAPA, -1)
        return jnp.dot(images, images.T, preferred_element_type=jnp.float32)

    alpha_gram = lax.map(alpha_target, (alpha_coupling.reshape(NA, CAPA, TILE, TILE), alpha_source.reshape(NA, CAPA), alpha_count))
    gamma_alpha = pair_density(alpha_gram, alpha_pair)

    beta_blocks = civec.reshape(NA * TILE, NB, TILE)

    def beta_target(inputs):
        couplings, sources, filled = inputs
        picked = jnp.take(beta_blocks, sources.astype(jnp.int32), axis=1).astype(jnp.float32)
        images = jnp.einsum('rsj,skj->srk', picked, couplings.astype(jnp.float32))
        occupied = (jnp.arange(CAPB, dtype=jnp.int32) < filled).astype(jnp.float32)
        images = (images * occupied[:, None, None]).astype(jnp.bfloat16).reshape(CAPB, -1)
        return jnp.dot(images, images.T, preferred_element_type=jnp.float32)

    beta_gram = lax.map(beta_target, (beta_coupling.reshape(NB, CAPB, TILE, TILE), beta_source.reshape(NB, CAPB), beta_count))
    gamma_beta = pair_density(beta_gram, beta_pair)
    return jnp.stack([gamma_alpha, gamma_beta])
```

```python
import functools

import jax
import jax.numpy as jnp
from jax import lax
from jax.experimental import pallas as pl
from jax.experimental.pallas import tpu as pltpu
from jax.sharding import PartitionSpec as P

NPAIR = 784
MESH = pl.DeviceIdType.MESH
F32 = jnp.float32
BF16 = jnp.bfloat16
LANES = 128
ROWT = 16


def up(n, m):
    return -(-n // m) * m


def dot_nt(x, y):
    return lax.dot_general(x, y, (((1,), (1,)), ((), ())), preferred_element_type=F32)


def dot_nn(x, y):
    return jnp.dot(x, y, preferred_element_type=F32)


def halves(x):
    hi = x.astype(BF16)
    return hi, (x - hi.astype(F32)).astype(BF16)


def iota(shape, dim):
    return lax.broadcasted_iota(jnp.int32, shape, dim)


def kernel(
    cfg, civec, acoup_hbm, asrc, apair, acnt, bcoup_hbm, bsrc, bpair, bcnt, out, *scratch
):
    na, nb, no, chunks, capa, capb, ta, tb, width, cols = cfg
    nbo = nb * no
    nq = len(chunks)
    panels = scratch[:nq]
    (
        acol, acoup, bcoup, ybuf, yabuf, vb, va, pall, gloc, rsbuf, exbuf, gsum,
        lsem, psem, xs, xr, os_, or_, fs, fr, als, alr, ps, pr, rss, rsr, exs, exr, ags, agr,
    ) = scratch[nq:]
    a = lax.axis_index("alpha")
    b = lax.axis_index("beta")
    o = lax.axis_index("orb")
    bo = b * no + o
    other = 1 - o
    row0 = [sum(chunks[:q]) for q in range(nq)]

    wide = cols // LANES

    def section(q, which):
        return panels[q].at[pl.ds(which * wide, wide)]

    def remote(src, dst, ss, rs, dev):
        return pltpu.make_async_remote_copy(
            src_ref=src, dst_ref=dst, send_sem=ss, recv_sem=rs,
            device_id=dev, device_id_type=MESH,
        )

    local = [
        [
            pltpu.make_async_copy(
                civec.at[row0[q] // LANES, pl.ds(row0[q] % LANES, chunks[q]), pl.ds(i * LANES, LANES)],
                panels[q].at[bo * wide + i], psem.at[q, i])
            for i in range(wide)
        ]
        for q in range(nq)
    ]
    bcopy = pltpu.make_async_copy(bcoup_hbm, bcoup, lsem.at[0])
    acopy = pltpu.make_async_copy(acoup_hbm, acoup, lsem.at[1])
    tall = civec.shape[0]
    ownrows = acol.at[pl.ds(a * tall, tall)]
    owncols = pltpu.make_async_copy(
        civec.at[:, :, pl.ds(pl.multiple_of(a * width, LANES), width)], ownrows, lsem.at[2])
    ownpair = pltpu.make_async_copy(bpair, pall.at[bo], lsem.at[3])

    barrier = pltpu.get_barrier_semaphore()
    for d in range(1, na):
        pl.semaphore_signal(barrier, inc=1, device_id={"alpha": lax.rem(a + d, na)}, device_id_type=MESH)
    for d in range(1, nbo):
        peer = lax.rem(bo + d, nbo)
        pl.semaphore_signal(
            barrier, inc=1,
            device_id={"beta": lax.div(peer, no), "orb": lax.rem(peer, no)}, device_id_type=MESH)
    for q in range(nq):
        for c in local[q]:
            c.start()
    ownpair.start()
    owncols.start()
    bcopy.start()
    acopy.start()
    pl.semaphore_wait(barrier, na - 1 + nbo - 1)

    xcopies, ocopies, fcopies, acopies, pcopies = {}, {}, {}, [], []
    for q in range(nq):
        for c in local[q]:
            c.wait()
        mine = section(q, bo)
        for d in range(1, nb):
            c = remote(mine, mine, xs.at[q, d], xr.at[q, d],
                       {"beta": lax.rem(b + d, nb)})
            c.start()
            xcopies[q, d] = c
        if q == 0:
            for d in range(1, na):
                peer = lax.rem(a + d, na)
                c = remote(
                    civec.at[:, :, pl.ds(pl.multiple_of(peer * width, LANES), width)], ownrows,
                    als.at[d], alr.at[d], {"alpha": peer})
                c.start()
                acopies.append(c)
        c = remote(mine, mine, os_.at[q], or_.at[q], {"orb": other})
        c.start()
        ocopies[q] = c
    for d in range(1, nbo):
        peer = lax.rem(bo + d, nbo)
        c = remote(bpair, pall.at[bo], ps.at[d], pr.at[d],
                   {"beta": lax.div(peer, no), "orb": lax.rem(peer, no)})
        c.start()
        pcopies.append(c)

    vb[...] = jnp.zeros_like(vb)
    va[...] = jnp.zeros_like(va)
    gloc[...] = jnp.zeros_like(gloc)
    yabuf[...] = jnp.zeros_like(yabuf)

    def forward(q):
        for d in range(1, nb):
            xcopies[q, d].wait_recv()
            sect = section(q, lax.rem(b - d + nb, nb) * no + o)
            c = remote(sect, sect, fs.at[q, d], fr.at[q, d], {"orb": other})
            c.start()
            fcopies[q, d] = c

    def arrive(q):
        ocopies[q].wait_recv()
        for d in range(1, nb):
            fcopies[q, d].wait_recv()

    ry = capb * ROWT
    keep_b = lax.rem(iota((ry, ry), 0), ROWT) == lax.rem(iota((ry, ry), 1), ROWT)

    def beta_chunk(q):
        n = chunks[q]

        @pl.loop(0, tb)
        def _(u):
            for k in range(capb):
                s = u * capb + k
                img = dot_nt(panels[q][bsrc[s]], bcoup[s]).astype(BF16)
                for j in range(n // ROWT):
                    ybuf[k * ROWT:(k + 1) * ROWT, j * LANES:(j + 1) * LANES] = img[j * ROWT:(j + 1) * ROWT]
            y = ybuf[:, : n // ROWT * LANES]
            z = jnp.where(keep_b, dot_nt(y, y), 0.0)
            vb[u] += z.reshape(capb, ROWT, ry).sum(axis=1)

    slots_a = 8
    ra = slots_a * ROWT
    keep_a = lax.rem(iota((ra, ra), 0), ROWT) == lax.rem(iota((ra, ra), 1), ROWT)

    def alpha_all():
        @pl.loop(0, ta)
        def _(t):
            for k in range(capa):
                s = t * capa + k
                img = dot_nn(acoup[s], acol[asrc[s]]).astype(BF16)
                for j in range(LANES // ROWT):
                    yabuf[k * ROWT:(k + 1) * ROWT, j * width:(j + 1) * width] = img[j * ROWT:(j + 1) * ROWT]
            y = yabuf[...]
            z = jnp.where(keep_a, dot_nt(y, y), 0.0)
            va[t] = z.reshape(slots_a, ROWT, ra).sum(axis=1)

    forward(0)
    bcopy.wait()
    for q in range(nq):
        arrive(q)
        if q == nq - 1:
            break
        beta_chunk(q)
        forward(q + 1)
        if q == nq - 2:
            acopy.wait()
            owncols.wait()
            for c in acopies:
                c.wait_recv()
            alpha_all()
    beta_chunk(nq - 1)

    pb = LANES // capb
    gb = []
    for g in range(tb // pb):
        total = jnp.zeros((capb, LANES), F32)
        for i in range(pb):
            pick = (iota((ry, LANES), 1) == i * capb + lax.div(iota((ry, LANES), 0), ROWT)).astype(BF16)
            hi, lo = halves(vb[g * pb + i])
            total += dot_nn(hi, pick) + dot_nn(lo, pick)
        cnt = bcnt[g:g + 1, :]
        lane = lax.rem(iota((capb, LANES), 1), capb)
        gb.append(jnp.where((iota((capb, LANES), 0) < cnt) & (lane < cnt), total, 0.0))
    pa = LANES // slots_a
    ga = []
    for g in range(ta // pa):
        total = jnp.zeros((slots_a, LANES), F32)
        for i in range(pa):
            pick = (iota((ra, LANES), 1) == i * slots_a + lax.div(iota((ra, LANES), 0), ROWT)).astype(BF16)
            hi, lo = halves(va[g * pa + i])
            total += dot_nn(hi, pick) + dot_nn(lo, pick)
        cnt = acnt[g:g + 1, :]
        lane = lax.rem(iota((slots_a, LANES), 1), slots_a)
        ga.append(jnp.where((iota((slots_a, LANES), 0) < cnt) & (lane < cnt), total, 0.0))

    rb = capb * len(gb) // na
    rah = slots_a * len(ga) // na
    for j in range(na):
        lo = j * rb
        gloc[j, 0:rb, :] = gb[lo // capb][lo % capb:lo % capb + rb, :]
        lo = j * rah
        gloc[j, 4:4 + rah, :] = ga[lo // slots_a][lo % slots_a:lo % slots_a + rah, :]
    rcopies = []
    for d in range(1, na):
        peer = lax.rem(a + d, na)
        c = remote(gloc.at[peer], rsbuf.at[d], rss.at[d], rsr.at[d], {"alpha": peer})
        c.start()
        rcopies.append(c)
    piece = gloc[a]
    for d in range(1, na):
        rcopies[d - 1].wait_recv()
        piece += rsbuf[d]
    exbuf[a, bo] = piece
    ecopies = []
    for d in range(1, nbo):
        peer = lax.rem(bo + d, nbo)
        c = remote(exbuf.at[a, bo], exbuf.at[a, bo], exs.at[d], exr.at[d],
                   {"beta": lax.div(peer, no), "orb": lax.rem(peer, no)})
        c.start()
        ecopies.append(c)
    for c in ecopies:
        c.wait_recv()
    gcopies = []
    for d in range(1, na):
        c = remote(exbuf.at[a], exbuf.at[a], ags.at[d], agr.at[d], {"alpha": lax.rem(a + d, na)})
        c.start()
        gcopies.append(c)
    ownpair.wait()
    for c in pcopies:
        c.wait_recv()
    for c in gcopies:
        c.wait_recv()

    prows, qcols = out.shape[1], out.shape[2]
    pp, qq = up(prows, 16), up(qcols, LANES)
    p0, q0 = a * prows, bo * qcols

    def density(pairs, grams, size):
        total = jnp.zeros((pp, qq), F32)
        same = lax.div(iota((LANES, LANES), 0), size) == lax.div(iota((LANES, LANES), 1), size)
        for pair, gram in zip(pairs, grams):
            left = (iota((pp, LANES), 0) + p0 == pair).astype(BF16)
            right = (iota((qq, LANES), 0) + q0 == pair).astype(BF16)
            blocks = jnp.where(same, jnp.concatenate([gram] * (LANES // size), axis=0), 0.0)
            hi, lo = halves(blocks)
            hi, lo = halves(dot_nn(right, hi) + dot_nn(right, lo))
            total += dot_nt(left, hi) + dot_nt(left, lo)
        return total[:prows, :qcols]

    for j in range(na):
        for m in range(nbo):
            gsum[m, j * rb:(j + 1) * rb, :] = exbuf[j, m, 0:rb, :]
        ones = exbuf[j, 0, 4:4 + rah, :]
        for m in range(1, nbo):
            ones += exbuf[j, m, 4:4 + rah, :]
        gsum[nbo, j * rah:(j + 1) * rah, :] = ones
    out[0] = density(
        [apair[g:g + 1, :] for g in range(len(ga))],
        [gsum[nbo, g * slots_a:(g + 1) * slots_a, :] for g in range(len(ga))], slots_a)
    out[1] = density(
        [pall[m, g:g + 1, :] for m in range(nbo) for g in range(len(gb))],
        [gsum[m, g * capb:(g + 1) * capb, :] for m in range(nbo) for g in range(len(gb))], capb)

    for group in (list(xcopies.values()), list(ocopies.values()), list(fcopies.values()),
                  acopies, pcopies, rcopies, ecopies, gcopies):
        for c in group:
            c.wait_send()


def body(mesh, civec, acoup, asrc, apair, acnt, bcoup, bsrc, bpair, bcnt):
    na, nb, no = mesh.shape["alpha"], mesh.shape["beta"], mesh.shape["orb"]
    nbo = nb * no
    rows, cols = civec.shape
    ta, tb = acnt.shape[0], bcnt.shape[0]
    capa, capb = asrc.shape[0] // ta, bsrc.shape[0] // tb
    width = cols // na
    chunks = (rows // 2, rows // 2)
    nq = len(chunks)
    slots_a = 8
    apad = jnp.pad(apair.reshape(ta, capa), ((0, 0), (0, slots_a - capa)), constant_values=-1)
    apad = apad.reshape(-1, LANES)
    acnts = jnp.repeat(acnt, slots_a).reshape(-1, LANES)
    bcnts = jnp.repeat(bcnt, capb).reshape(-1, LANES)
    bpairs = bpair.reshape(-1, LANES)
    groups = bpairs.shape[0]
    cfg = (na, nb, no, chunks, capa, capb, ta, tb, width, cols)
    anyspace = pl.BlockSpec(memory_space=pl.ANY)
    vmem = pl.BlockSpec(memory_space=pltpu.VMEM)
    smem = pl.BlockSpec(memory_space=pltpu.SMEM)
    dma = pltpu.SemaphoreType.DMA
    return pl.pallas_call(
        functools.partial(kernel, cfg),
        out_shape=jax.ShapeDtypeStruct((2, NPAIR // na, NPAIR // nbo), F32),
        in_specs=[anyspace, anyspace, smem, vmem, vmem, anyspace, smem, vmem, vmem],
        out_specs=vmem,
        scratch_shapes=[pltpu.VMEM((cols * nbo // LANES, n, LANES), BF16) for n in chunks] + [
            pltpu.VMEM((rows * na // LANES, LANES, width), BF16),
            pltpu.VMEM(acoup.shape, BF16),
            pltpu.VMEM(bcoup.shape, BF16),
            pltpu.VMEM((capb * ROWT, max(chunks) // ROWT * LANES), BF16),
            pltpu.VMEM((slots_a * ROWT, LANES // ROWT * width), BF16),
            pltpu.VMEM((tb, capb, capb * ROWT), F32),
            pltpu.VMEM((ta, slots_a, slots_a * ROWT), F32),
            pltpu.VMEM((nbo, groups, LANES), jnp.int32),
            pltpu.VMEM((na, 8, LANES), F32),
            pltpu.VMEM((na, 8, LANES), F32),
            pltpu.VMEM((na, nbo, 8, LANES), F32),
            pltpu.VMEM((nbo + 1, groups * capb, LANES), F32),
            dma((4,)), dma((nq, cols // LANES)),
            dma((nq, nb)), dma((nq, nb)), dma((nq,)), dma((nq,)), dma((nq, nb)), dma((nq, nb)),
            dma((na,)), dma((na,)), dma((nbo,)), dma((nbo,)),
            dma((na,)), dma((na,)), dma((nbo,)), dma((nbo,)), dma((na,)), dma((na,)),
        ],
        compiler_params=pltpu.CompilerParams(
            collective_id=0, has_side_effects=True, vmem_limit_bytes=48 * 1024 * 1024),
    )(civec.reshape(-1, LANES, cols), acoup, asrc, apad, acnts, bcoup, bsrc, bpairs, bcnts)


def solution(mesh):
    return jax.shard_map(
        functools.partial(body, mesh),
        mesh=mesh,
        in_specs=(
            P(("frag", "alpha"), ("beta", "orb")),
            P("frag", None, None),
            P("frag"),
            P("frag"),
            P("frag"),
            P(("frag", "beta", "orb"), None, None),
            P(("frag", "beta", "orb")),
            P(("frag", "beta", "orb")),
            P(("frag", "beta", "orb")),
        ),
        out_specs=P("frag", "alpha", ("beta", "orb")),
        check_vma=False,
    )
```

```python
import functools

import jax
import jax.numpy as jnp
from jax import lax
from jax.experimental import pallas as pl
from jax.experimental.pallas import tpu as pltpu
from jax.sharding import PartitionSpec as P

NPAIR = 784
MESH = pl.DeviceIdType.MESH
F32 = jnp.float32
BF16 = jnp.bfloat16
LANES = 128
ROWT = 16


def up(n, m):
    return -(-n // m) * m


def dot_nt(x, y):
    return lax.dot_general(x, y, (((1,), (1,)), ((), ())), preferred_element_type=F32)


def dot_nn(x, y):
    return jnp.dot(x, y, preferred_element_type=F32)


def halves(x):
    hi = x.astype(BF16)
    return hi, (x - hi.astype(F32)).astype(BF16)


def iota(shape, dim):
    return lax.broadcasted_iota(jnp.int32, shape, dim)


def kernel(
    cfg, civec, acoup_hbm, asrc_h, apair_h, acnt_h, bcoup_hbm, bsrc_h, bpair_h, bcnt_h, out, *scratch
):
    na, nb, no, chunks, ahead, capa, capb, ta, tb, width, cols = cfg
    nbo = nb * no
    nq = len(chunks)
    nc = width // LANES
    panels, acols = scratch[:nq], scratch[nq:nq + nc]
    (
        asrc, apairs, acnts, bsrc, bpairs, bcnts,
        acoup, bcoup, ybuf0, ybuf1, yabuf0, yabuf1, vb, va, pall, pbuf, qbuf, gloc, rsbuf, exbuf, gsum,
        lsem, csem, psem, xs, xr, os_, or_, fs, fr, als, alr, ps, pr, rss, rsr, exs, exr, ags, agr,
    ) = scratch[nq + nc:]
    a = lax.axis_index("alpha")
    b = lax.axis_index("beta")
    o = lax.axis_index("orb")
    bo = b * no + o
    other = 1 - o
    row0 = [sum(chunks[:q]) for q in range(nq)]

    wide = cols // LANES

    def section(q, which):
        return panels[q].at[pl.ds(which * wide, wide)]

    def remote(src, dst, ss, rs, dev):
        return pltpu.make_async_remote_copy(
            src_ref=src, dst_ref=dst, send_sem=ss, recv_sem=rs,
            device_id=dev, device_id_type=MESH,
        )

    local = [
        [
            pltpu.make_async_copy(
                civec.at[row0[q] // LANES, pl.ds(row0[q] % LANES, chunks[q]), pl.ds(i * LANES, LANES)],
                panels[q].at[bo * wide + i], psem.at[q, i])
            for i in range(wide)
        ]
        for q in range(nq)
    ]
    bcopy = pltpu.make_async_copy(bcoup_hbm, bcoup, lsem.at[0])
    acopy = pltpu.make_async_copy(acoup_hbm, acoup, lsem.at[1])
    tall = civec.shape[0]
    ownrows = pl.ds(a * tall, tall)

    def piece_of(which, c):
        return civec.at[:, :, pl.ds(pl.multiple_of(which * width + c * LANES, LANES), LANES)]

    owncols = [
        pltpu.make_async_copy(piece_of(a, c), acols[c].at[ownrows], csem.at[c]) for c in range(nc)
    ]
    lists = [
        pltpu.make_async_copy(src, dst, lsem.at[2 + i])
        for i, (src, dst) in enumerate((
            (asrc_h, asrc), (apair_h, apairs), (acnt_h, acnts),
            (bsrc_h, bsrc), (bpair_h, bpairs), (bcnt_h, bcnts)))
    ]

    barrier = pltpu.get_barrier_semaphore()
    for d in range(1, na):
        pl.semaphore_signal(barrier, inc=1, device_id={"alpha": lax.rem(a + d, na)}, device_id_type=MESH)
    for d in range(1, nbo):
        peer = lax.rem(bo + d, nbo)
        pl.semaphore_signal(
            barrier, inc=1,
            device_id={"beta": lax.div(peer, no), "orb": lax.rem(peer, no)}, device_id_type=MESH)
    for q in range(nq):
        for c in local[q]:
            c.start()
    for c in lists + owncols:
        c.start()
    bcopy.start()
    acopy.start()
    pl.semaphore_wait(barrier, na - 1 + nbo - 1)

    xcopies, ocopies, fcopies, acopies, pcopies = {}, {}, {}, {}, []

    def send_chunk(q):
        for c in local[q]:
            c.wait()
        mine = section(q, bo)
        for d in range(1, nb):
            c = remote(mine, mine, xs.at[q, d], xr.at[q, d], {"beta": lax.rem(b + d, nb)})
            c.start()
            xcopies[q, d] = c
        c = remote(mine, mine, os_.at[q], or_.at[q], {"orb": other})
        c.start()
        ocopies[q] = c

    def send_cols(c):
        for d in range(na - 1, 0, -1):
            peer = lax.rem(a + d, na)
            copy = remote(piece_of(peer, c), acols[c].at[ownrows], als.at[c, d], alr.at[c, d], {"alpha": peer})
            copy.start()
            acopies[c, d] = copy

    send_chunk(0)
    for c in range(nc):
        send_cols(c)

    def lane_row(values):
        lanes = iota((1, LANES), 1)
        row = jnp.full((1, LANES), -1, jnp.int32)
        for lane, value in values:
            row = jnp.where(lanes == lane, value, row)
        return row

    def span_row(values, size):
        lanes = lax.div(iota((1, LANES), 1), size)
        row = jnp.zeros((1, LANES), jnp.int32)
        for i, value in enumerate(values):
            row = jnp.where(lanes == i, value, row)
        return row

    slots_a = 8
    pa, pb = LANES // slots_a, LANES // capb
    na_g, nb_g = ta // pa, tb // pb
    for c in lists:
        c.wait()
    for g in range(nb_g):
        pall[bo, g:g + 1, :] = lane_row([(i, bpairs[g * LANES + i]) for i in range(LANES)])
    apair = [
        lane_row([(i * slots_a + k, apairs[(g * pa + i) * capa + k]) for i in range(pa) for k in range(capa)])
        for g in range(na_g)
    ]
    acnt = [span_row([acnts[g * pa + i] for i in range(pa)], slots_a) for g in range(na_g)]
    bcnt = [span_row([bcnts[g * pb + i] for i in range(pb)], capb) for g in range(nb_g)]
    for d in range(1, nbo):
        peer = lax.rem(bo + d, nbo)
        c = remote(pall.at[bo], pall.at[bo], ps.at[d], pr.at[d],
                   {"beta": lax.div(peer, no), "orb": lax.rem(peer, no)})
        c.start()
        pcopies.append(c)

    for q in range(1, min(ahead, nq)):
        send_chunk(q)

    vb[...] = jnp.zeros_like(vb)
    va[...] = jnp.zeros_like(va)
    gloc[...] = jnp.zeros_like(gloc)
    yabuf0[...] = jnp.zeros_like(yabuf0)
    yabuf1[...] = jnp.zeros_like(yabuf1)

    def forward(q):
        for d in range(1, nb):
            xcopies[q, d].wait_recv()
            sect = section(q, lax.rem(b - d + nb, nb) * no + o)
            c = remote(sect, sect, fs.at[q, d], fr.at[q, d], {"orb": other})
            c.start()
            fcopies[q, d] = c

    def arrive(q):
        ocopies[q].wait_recv()
        for d in range(1, nb):
            fcopies[q, d].wait_recv()

    ry = capb * ROWT
    keep_b = lax.rem(iota((ry, ry), 0), ROWT) == lax.rem(iota((ry, ry), 1), ROWT)

    def beta_chunk(q):
        n = chunks[q]

        def images(u, ybuf):
            for k in range(capb):
                s = u * capb + k
                img = dot_nn(panels[q][bsrc[s]], bcoup[s]).astype(BF16)
                for j in range(n // ROWT):
                    ybuf[k * ROWT:(k + 1) * ROWT, j * LANES:(j + 1) * LANES] = img[j * ROWT:(j + 1) * ROWT]

        def gram(u, ybuf):
            y = ybuf[:, : n // ROWT * LANES]
            z = jnp.where(keep_b, dot_nt(y, y), 0.0)
            vb[u] += z.reshape(capb, ROWT, ry).sum(axis=1)

        images(0, ybuf0)

        @pl.loop(0, tb // 2)
        def _(i):
            images(2 * i + 1, ybuf1)
            gram(2 * i, ybuf0)
            images(lax.rem(2 * i + 2, tb), ybuf0)
            gram(2 * i + 1, ybuf1)

    ra = slots_a * ROWT
    keep_a = lax.rem(iota((ra, ra), 0), ROWT) == lax.rem(iota((ra, ra), 1), ROWT)

    def alpha_chunk(c):
        acopies_c = [acopies[c, d] for d in range(1, na)]
        owncols[c].wait()
        for copy in acopies_c:
            copy.wait_recv()

        def images(t, ybuf):
            for k in range(capa):
                s = t * capa + k
                img = dot_nn(acoup[s], acols[c][asrc[s]]).astype(BF16)
                for j in range(LANES // ROWT):
                    ybuf[k * ROWT:(k + 1) * ROWT, j * LANES:(j + 1) * LANES] = img[j * ROWT:(j + 1) * ROWT]

        def gram(t, ybuf):
            y = ybuf[...]
            z = jnp.where(keep_a, dot_nt(y, y), 0.0)
            va[t] += z.reshape(slots_a, ROWT, ra).sum(axis=1)

        images(0, yabuf0)

        @pl.loop(0, ta // 2)
        def _(i):
            images(2 * i + 1, yabuf1)
            gram(2 * i, yabuf0)
            images(lax.rem(2 * i + 2, ta), yabuf0)
            gram(2 * i + 1, yabuf1)

    bcopy.wait()

    @pl.loop(0, bcoup.shape[0] // 8)
    def _(i):
        for k in range(8):
            bcoup[i * 8 + k] = bcoup[i * 8 + k].T

    prows, qcols = out.shape[1], out.shape[2]
    pp, qq = up(prows, 16), up(qcols, LANES)
    p0, q0 = a * prows, bo * qcols
    ngb = nbo * nb_g
    def onehots():
        for c in pcopies:
            c.wait_recv()
        for g in range(ngb + na_g):
            pair = pall[g // nb_g, g % nb_g:g % nb_g + 1, :] if g < ngb else apair[g - ngb]
            pbuf[:, g * LANES:(g + 1) * LANES] = (iota((pp, LANES), 0) + p0 == pair).astype(BF16)
            qbuf[g] = (iota((qq, LANES), 0) + q0 == pair).astype(F32).T.astype(BF16)

    done_a = 0
    for q in range(nq):
        if q == nq - 1:
            onehots()
            acopy.wait()
            while done_a < nc - 1:
                alpha_chunk(done_a)
                done_a += 1
        forward(q)
        if q + ahead < nq:
            send_chunk(q + ahead)
        if q == nq - 1:
            while done_a < nc:
                alpha_chunk(done_a)
                done_a += 1
        arrive(q)
        beta_chunk(q)

    def side_by_side(v, size, counts):
        n = LANES // size
        pick = lax.rem(iota((size * ROWT, LANES), 1), size) == lax.div(iota((size * ROWT, LANES), 0), ROWT)
        hi, lo = halves(v[...].reshape(-1, size * ROWT))
        total = dot_nn(jnp.concatenate([hi, lo], axis=1), jnp.concatenate([pick.astype(BF16)] * 2, axis=0))
        lanes, slot = iota((size, LANES), 1), iota((size, LANES), 0)
        grams = []
        for g, cnt in enumerate(counts):
            gram = jnp.zeros((size, LANES), F32)
            for i in range(n):
                r = (g * n + i) * size
                gram = jnp.where(lax.div(lanes, size) == i, total[r:r + size], gram)
            grams.append(jnp.where((slot < cnt) & (lax.rem(lanes, size) < cnt), gram, 0.0))
        return grams

    gb = side_by_side(vb, capb, bcnt)
    ga = side_by_side(va, slots_a, acnt)

    rb = capb * len(gb) // na
    rah = slots_a * len(ga) // na
    for j in range(na):
        lo = j * rb
        gloc[j, 0:rb, :] = gb[lo // capb][lo % capb:lo % capb + rb, :]
        lo = j * rah
        gloc[j, 4:4 + rah, :] = ga[lo // slots_a][lo % slots_a:lo % slots_a + rah, :]
    rcopies = []
    for d in range(1, na):
        peer = lax.rem(a + d, na)
        c = remote(gloc.at[peer], rsbuf.at[d], rss.at[d], rsr.at[d], {"alpha": peer})
        c.start()
        rcopies.append(c)
    piece = gloc[a]
    for d in range(1, na):
        rcopies[d - 1].wait_recv()
        piece += rsbuf[d]
    exbuf[a, bo] = piece
    ecopies = []
    for d in range(1, nbo):
        peer = lax.rem(bo + d, nbo)
        c = remote(exbuf.at[a, bo], exbuf.at[a, bo], exs.at[d], exr.at[d],
                   {"beta": lax.div(peer, no), "orb": lax.rem(peer, no)})
        c.start()
        ecopies.append(c)
    for c in ecopies:
        c.wait_recv()
    gcopies = []
    for d in range(1, na):
        c = remote(exbuf.at[a], exbuf.at[a], ags.at[d], agr.at[d], {"alpha": lax.rem(a + d, na)})
        c.start()
        gcopies.append(c)
    for c in gcopies:
        c.wait_recv()

    def density(grams, first, size):
        same = lax.div(iota((LANES, LANES), 0), size) == lax.div(iota((LANES, LANES), 1), size)
        his, los = [], []
        for i, gram in enumerate(grams):
            blocks = jnp.where(same, jnp.concatenate([gram] * (LANES // size), axis=0), 0.0)
            hi, lo = halves(blocks)
            right = qbuf[first + i]
            hi, lo = halves(dot_nn(
                jnp.concatenate([hi, lo], axis=1), jnp.concatenate([right, right], axis=0)))
            his.append(hi)
            los.append(lo)
        left = pbuf[:, first * LANES:(first + len(grams)) * LANES]
        total = dot_nn(left, jnp.concatenate(his, axis=0)) + dot_nn(left, jnp.concatenate(los, axis=0))
        return total[:prows, :qcols]

    for j in range(na):
        for m in range(nbo):
            gsum[m, j * rb:(j + 1) * rb, :] = exbuf[j, m, 0:rb, :]
        ones = exbuf[j, 0, 4:4 + rah, :]
        for m in range(1, nbo):
            ones += exbuf[j, m, 4:4 + rah, :]
        gsum[nbo, j * rah:(j + 1) * rah, :] = ones
    out[0] = density([gsum[nbo, g * slots_a:(g + 1) * slots_a, :] for g in range(na_g)], ngb, slots_a)
    out[1] = density(
        [gsum[m, g * capb:(g + 1) * capb, :] for m in range(nbo) for g in range(nb_g)], 0, capb)

    for group in (list(xcopies.values()), list(ocopies.values()), list(fcopies.values()),
                  list(acopies.values()), pcopies, rcopies, ecopies, gcopies):
        for c in group:
            c.wait_send()


def body(mesh, civec, acoup, asrc, apair, acnt, bcoup, bsrc, bpair, bcnt):
    na, nb, no = mesh.shape["alpha"], mesh.shape["beta"], mesh.shape["orb"]
    nbo = nb * no
    rows, cols = civec.shape
    ta, tb = acnt.shape[0], bcnt.shape[0]
    capa, capb = asrc.shape[0] // ta, bsrc.shape[0] // tb
    width = cols // na
    chunks = (rows // 2, rows // 2)
    ahead = len(chunks)
    nq, nc = len(chunks), width // LANES
    slots_a = 8
    groups, groups_a = bpair.shape[0] // LANES, ta * slots_a // LANES
    cfg = (na, nb, no, chunks, ahead, capa, capb, ta, tb, width, cols)
    anyspace = pl.BlockSpec(memory_space=pl.ANY)
    vmem = pl.BlockSpec(memory_space=pltpu.VMEM)
    dma = pltpu.SemaphoreType.DMA
    return pl.pallas_call(
        functools.partial(kernel, cfg),
        out_shape=jax.ShapeDtypeStruct((2, NPAIR // na, NPAIR // nbo), F32),
        in_specs=[anyspace] * 9,
        out_specs=vmem,
        scratch_shapes=[pltpu.VMEM((cols * nbo // LANES, n, LANES), BF16) for n in chunks] + [
            pltpu.VMEM((rows * na // LANES, LANES, LANES), BF16) for _ in range(nc)] + [
            pltpu.SMEM(x.shape, jnp.int32) for x in (asrc, apair, acnt, bsrc, bpair, bcnt)] + [
            pltpu.VMEM(acoup.shape, BF16),
            pltpu.VMEM(bcoup.shape, BF16),
            pltpu.VMEM((capb * ROWT, max(chunks) // ROWT * LANES), BF16),
            pltpu.VMEM((capb * ROWT, max(chunks) // ROWT * LANES), BF16),
            pltpu.VMEM((slots_a * ROWT, LANES // ROWT * LANES), BF16),
            pltpu.VMEM((slots_a * ROWT, LANES // ROWT * LANES), BF16),
            pltpu.VMEM((tb, capb, capb * ROWT), F32),
            pltpu.VMEM((ta, slots_a, slots_a * ROWT), F32),
            pltpu.VMEM((nbo, groups, LANES), jnp.int32),
            pltpu.VMEM((up(NPAIR // na, 16), (nbo * groups + groups_a) * LANES), BF16),
            pltpu.VMEM((nbo * groups + groups_a, LANES, up(NPAIR // nbo, LANES)), BF16),
            pltpu.VMEM((na, 8, LANES), F32),
            pltpu.VMEM((na, 8, LANES), F32),
            pltpu.VMEM((na, nbo, 8, LANES), F32),
            pltpu.VMEM((nbo + 1, groups * capb, LANES), F32),
            dma((8,)), dma((nc,)), dma((nq, cols // LANES)),
            dma((nq, nb)), dma((nq, nb)), dma((nq,)), dma((nq,)), dma((nq, nb)), dma((nq, nb)),
            dma((nc, na)), dma((nc, na)), dma((nbo,)), dma((nbo,)),
            dma((na,)), dma((na,)), dma((nbo,)), dma((nbo,)), dma((na,)), dma((na,)),
        ],
        compiler_params=pltpu.CompilerParams(
            collective_id=0, has_side_effects=True, vmem_limit_bytes=60 * 1024 * 1024),
    )(civec.reshape(-1, LANES, cols), acoup, asrc, apair, acnt, bcoup, bsrc, bpair, bcnt)


def solution(mesh):
    return jax.shard_map(
        functools.partial(body, mesh),
        mesh=mesh,
        in_specs=(
            P(("frag", "alpha"), ("beta", "orb")),
            P("frag", None, None),
            P("frag"),
            P("frag"),
            P("frag"),
            P(("frag", "beta", "orb"), None, None),
            P(("frag", "beta", "orb")),
            P(("frag", "beta", "orb")),
            P(("frag", "beta", "orb")),
        ),
        out_specs=P("frag", "alpha", ("beta", "orb")),
        check_vma=False,
    )
```

```python
import functools

import jax
import jax.numpy as jnp
from jax import lax
from jax.experimental import pallas as pl
from jax.experimental.pallas import tpu as pltpu
from jax.sharding import PartitionSpec as P

NPAIR = 784
MESH = pl.DeviceIdType.MESH
F32 = jnp.float32
BF16 = jnp.bfloat16
LANES = 128
ROWT = 16


def up(n, m):
    return -(-n // m) * m


def dot_nt(x, y):
    return lax.dot_general(x, y, (((1,), (1,)), ((), ())), preferred_element_type=F32)


def dot_nn(x, y):
    return jnp.dot(x, y, preferred_element_type=F32)


def halves(x):
    hi = x.astype(BF16)
    return hi, (x - hi.astype(F32)).astype(BF16)


def iota(shape, dim):
    return lax.broadcasted_iota(jnp.int32, shape, dim)


def kernel(
    cfg, civec, acoup_hbm, asrc_h, apair_h, acnt_h, bcoup_hbm, bsrc_h, bpair_h, bcnt_h, out, *scratch
):
    na, nb, no, chunks, ahead, capa, capb, ta, tb, width, cols = cfg
    nbo = nb * no
    nq = len(chunks)
    nc = width // LANES
    panels, acols = scratch[:nq], scratch[nq:nq + nc]
    (
        asrc, apairs, acnts, bsrc, bpairs, bcnts,
        acoup, bcoup, ybuf0, ybuf1, yabuf0, yabuf1, vb, va, pall, pbuf, qbuf, gloc, rsbuf, exbuf, gsum,
        lsem, csem, psem, xs, xr, os_, or_, fs, fr, als, alr, ps, pr, rss, rsr, exs, exr,
    ) = scratch[nq + nc:]
    a = lax.axis_index("alpha")
    b = lax.axis_index("beta")
    o = lax.axis_index("orb")
    bo = b * no + o
    other = 1 - o
    row0 = [sum(chunks[:q]) for q in range(nq)]

    wide = cols // LANES

    def section(q, which):
        return panels[q].at[pl.ds(which * wide, wide)]

    def remote(src, dst, ss, rs, dev):
        return pltpu.make_async_remote_copy(
            src_ref=src, dst_ref=dst, send_sem=ss, recv_sem=rs,
            device_id=dev, device_id_type=MESH,
        )

    local = [
        [
            pltpu.make_async_copy(
                civec.at[row0[q] // LANES, pl.ds(row0[q] % LANES, chunks[q]), pl.ds(i * LANES, LANES)],
                panels[q].at[bo * wide + i], psem.at[q, i])
            for i in range(wide)
        ]
        for q in range(nq)
    ]
    bcopy = pltpu.make_async_copy(bcoup_hbm, bcoup, lsem.at[0])
    acopy = pltpu.make_async_copy(acoup_hbm, acoup, lsem.at[1])
    tall = civec.shape[0]
    ownrows = pl.ds(a * tall, tall)

    def piece_of(which, c):
        return civec.at[:, :, pl.ds(pl.multiple_of(which * width + c * LANES, LANES), LANES)]

    owncols = [
        pltpu.make_async_copy(piece_of(a, c), acols[c].at[ownrows], csem.at[c]) for c in range(nc)
    ]
    lists = [
        pltpu.make_async_copy(src, dst, lsem.at[2 + i])
        for i, (src, dst) in enumerate((
            (asrc_h, asrc), (apair_h, apairs), (acnt_h, acnts),
            (bsrc_h, bsrc), (bpair_h, bpairs), (bcnt_h, bcnts)))
    ]

    barrier = pltpu.get_barrier_semaphore()
    everyone = na * nbo

    def device(d):
        peer_a, peer = lax.rem(a + lax.div(d, nbo), na), lax.rem(bo + lax.rem(d, nbo), nbo)
        return {"alpha": peer_a, "beta": lax.div(peer, no), "orb": lax.rem(peer, no)}

    @pl.loop(1, everyone)
    def _(d):
        pl.semaphore_signal(barrier, inc=1, device_id=device(d), device_id_type=MESH)

    for q in range(nq):
        for c in local[q]:
            c.start()
    for c in lists + owncols:
        c.start()
    bcopy.start()
    acopy.start()
    pl.semaphore_wait(barrier, everyone - 1)

    xcopies, ocopies, fcopies, acopies, pcopies = {}, {}, {}, {}, []

    def send_chunk(q):
        for c in local[q]:
            c.wait()
        mine = section(q, bo)
        for d in range(1, nb):
            c = remote(mine, mine, xs.at[q, d], xr.at[q, d], {"beta": lax.rem(b + d, nb)})
            c.start()
            xcopies[q, d] = c
        c = remote(mine, mine, os_.at[q], or_.at[q], {"orb": other})
        c.start()
        ocopies[q] = c

    def send_cols(c):
        for d in range(na - 1, 0, -1):
            peer = lax.rem(a + d, na)
            copy = remote(piece_of(peer, c), acols[c].at[ownrows], als.at[c, d], alr.at[c, d], {"alpha": peer})
            copy.start()
            acopies[c, d] = copy

    send_chunk(0)
    for c in range(nc):
        send_cols(c)

    def lane_row(values):
        lanes = iota((1, LANES), 1)
        row = jnp.full((1, LANES), -1, jnp.int32)
        for lane, value in values:
            row = jnp.where(lanes == lane, value, row)
        return row

    def span_row(values, size):
        lanes = lax.div(iota((1, LANES), 1), size)
        row = jnp.zeros((1, LANES), jnp.int32)
        for i, value in enumerate(values):
            row = jnp.where(lanes == i, value, row)
        return row

    slots_a = 8
    pa, pb = LANES // slots_a, LANES // capb
    na_g, nb_g = ta // pa, tb // pb
    for c in lists:
        c.wait()
    for g in range(nb_g):
        pall[bo, g:g + 1, :] = lane_row([(i, bpairs[g * LANES + i]) for i in range(LANES)])
    apair = [
        lane_row([(i * slots_a + k, apairs[(g * pa + i) * capa + k]) for i in range(pa) for k in range(capa)])
        for g in range(na_g)
    ]
    acnt = [span_row([acnts[g * pa + i] for i in range(pa)], slots_a) for g in range(na_g)]
    bcnt = [span_row([bcnts[g * pb + i] for i in range(pb)], capb) for g in range(nb_g)]
    for d in range(1, nbo):
        peer = lax.rem(bo + d, nbo)
        c = remote(pall.at[bo], pall.at[bo], ps.at[d], pr.at[d],
                   {"beta": lax.div(peer, no), "orb": lax.rem(peer, no)})
        c.start()
        pcopies.append(c)

    for q in range(1, min(ahead, nq)):
        send_chunk(q)

    vb[...] = jnp.zeros_like(vb)
    va[...] = jnp.zeros_like(va)
    gloc[...] = jnp.zeros_like(gloc)
    yabuf0[...] = jnp.zeros_like(yabuf0)
    yabuf1[...] = jnp.zeros_like(yabuf1)

    def forward(q):
        for d in range(1, nb):
            xcopies[q, d].wait_recv()
            sect = section(q, lax.rem(b - d + nb, nb) * no + o)
            c = remote(sect, sect, fs.at[q, d], fr.at[q, d], {"orb": other})
            c.start()
            fcopies[q, d] = c

    def arrive(q):
        ocopies[q].wait_recv()
        for d in range(1, nb):
            fcopies[q, d].wait_recv()

    ry = capb * ROWT
    keep_b = lax.rem(iota((ry, ry), 0), ROWT) == lax.rem(iota((ry, ry), 1), ROWT)

    def beta_chunk(q):
        n = chunks[q]

        def images(u, ybuf):
            for k in range(capb):
                s = u * capb + k
                img = dot_nn(panels[q][bsrc[s]], bcoup[s]).astype(BF16)
                for j in range(n // ROWT):
                    ybuf[k * ROWT:(k + 1) * ROWT, j * LANES:(j + 1) * LANES] = img[j * ROWT:(j + 1) * ROWT]

        def gram(u, ybuf):
            y = ybuf[:, : n // ROWT * LANES]
            z = jnp.where(keep_b, dot_nt(y, y), 0.0)
            vb[u] += z.reshape(capb, ROWT, ry).sum(axis=1)

        images(0, ybuf0)

        @pl.loop(0, tb // 2)
        def _(i):
            images(2 * i + 1, ybuf1)
            gram(2 * i, ybuf0)
            images(lax.rem(2 * i + 2, tb), ybuf0)
            gram(2 * i + 1, ybuf1)

    ra = slots_a * ROWT
    keep_a = lax.rem(iota((ra, ra), 0), ROWT) == lax.rem(iota((ra, ra), 1), ROWT)

    def alpha_chunk(c):
        acopies_c = [acopies[c, d] for d in range(1, na)]
        owncols[c].wait()
        for copy in acopies_c:
            copy.wait_recv()

        def images(t, ybuf):
            for k in range(capa):
                s = t * capa + k
                img = dot_nn(acoup[s], acols[c][asrc[s]]).astype(BF16)
                for j in range(LANES // ROWT):
                    ybuf[k * ROWT:(k + 1) * ROWT, j * LANES:(j + 1) * LANES] = img[j * ROWT:(j + 1) * ROWT]

        def gram(t, ybuf):
            y = ybuf[...]
            z = jnp.where(keep_a, dot_nt(y, y), 0.0)
            va[t] += z.reshape(slots_a, ROWT, ra).sum(axis=1)

        images(0, yabuf0)

        @pl.loop(0, ta // 2)
        def _(i):
            images(2 * i + 1, yabuf1)
            gram(2 * i, yabuf0)
            images(lax.rem(2 * i + 2, ta), yabuf0)
            gram(2 * i + 1, yabuf1)

    bcopy.wait()

    @pl.loop(0, bcoup.shape[0] // 8)
    def _(i):
        for k in range(8):
            bcoup[i * 8 + k] = bcoup[i * 8 + k].T

    prows, qcols = out.shape[1], out.shape[2]
    pp, qq = up(prows, 16), up(qcols, LANES)
    p0, q0 = a * prows, bo * qcols
    ngb = nbo * nb_g
    def onehots():
        for c in pcopies:
            c.wait_recv()
        for g in range(ngb + na_g):
            pair = pall[g // nb_g, g % nb_g:g % nb_g + 1, :] if g < ngb else apair[g - ngb]
            pbuf[:, g * LANES:(g + 1) * LANES] = (iota((pp, LANES), 0) + p0 == pair).astype(BF16)
            qbuf[g] = (iota((qq, LANES), 0) + q0 == pair).astype(F32).T.astype(BF16)

    done_a = 0
    for q in range(nq):
        if q == nq - 1:
            onehots()
            acopy.wait()
            while done_a < nc - 1:
                alpha_chunk(done_a)
                done_a += 1
        forward(q)
        if q + ahead < nq:
            send_chunk(q + ahead)
        if q == nq - 1:
            while done_a < nc:
                alpha_chunk(done_a)
                done_a += 1
        arrive(q)
        beta_chunk(q)

    def side_by_side(v, size, counts):
        n = LANES // size
        pick = lax.rem(iota((size * ROWT, LANES), 1), size) == lax.div(iota((size * ROWT, LANES), 0), ROWT)
        hi, lo = halves(v[...].reshape(-1, size * ROWT))
        total = dot_nn(jnp.concatenate([hi, lo], axis=1), jnp.concatenate([pick.astype(BF16)] * 2, axis=0))
        lanes, slot = iota((size, LANES), 1), iota((size, LANES), 0)
        grams = []
        for g, cnt in enumerate(counts):
            gram = jnp.zeros((size, LANES), F32)
            for i in range(n):
                r = (g * n + i) * size
                gram = jnp.where(lax.div(lanes, size) == i, total[r:r + size], gram)
            grams.append(jnp.where((slot < cnt) & (lax.rem(lanes, size) < cnt), gram, 0.0))
        return grams

    gb = side_by_side(vb, capb, bcnt)
    ga = side_by_side(va, slots_a, acnt)

    rb = capb * len(gb) // na
    rah = slots_a * len(ga) // na
    for j in range(na):
        lo = j * rb
        gloc[j, 0:rb, :] = gb[lo // capb][lo % capb:lo % capb + rb, :]
        lo = j * rah
        gloc[j, 4:4 + rah, :] = ga[lo // slots_a][lo % slots_a:lo % slots_a + rah, :]
    rcopies = []
    for d in range(1, na):
        peer = lax.rem(a + d, na)
        c = remote(gloc.at[peer], rsbuf.at[d], rss.at[d], rsr.at[d], {"alpha": peer})
        c.start()
        rcopies.append(c)
    piece = gloc[a]
    for d in range(1, na):
        rcopies[d - 1].wait_recv()
        piece += rsbuf[d]
    exbuf[a, bo] = piece

    def spread(d):
        return remote(exbuf.at[a, bo], exbuf.at[a, bo], exs.at[d], exr.at[d], device(d))

    @pl.loop(1, everyone)
    def _(d):
        spread(d).start()

    @pl.loop(1, everyone)
    def _(d):
        spread(d).wait_recv()

    def density(grams, first, size):
        same = lax.div(iota((LANES, LANES), 0), size) == lax.div(iota((LANES, LANES), 1), size)
        his, los = [], []
        for i, gram in enumerate(grams):
            blocks = jnp.where(same, jnp.concatenate([gram] * (LANES // size), axis=0), 0.0)
            hi, lo = halves(blocks)
            right = qbuf[first + i]
            hi, lo = halves(dot_nn(
                jnp.concatenate([hi, lo], axis=1), jnp.concatenate([right, right], axis=0)))
            his.append(hi)
            los.append(lo)
        left = pbuf[:, first * LANES:(first + len(grams)) * LANES]
        total = dot_nn(left, jnp.concatenate(his, axis=0)) + dot_nn(left, jnp.concatenate(los, axis=0))
        return total[:prows, :qcols]

    for j in range(na):
        for m in range(nbo):
            gsum[m, j * rb:(j + 1) * rb, :] = exbuf[j, m, 0:rb, :]
        ones = exbuf[j, 0, 4:4 + rah, :]
        for m in range(1, nbo):
            ones += exbuf[j, m, 4:4 + rah, :]
        gsum[nbo, j * rah:(j + 1) * rah, :] = ones
    out[0] = density([gsum[nbo, g * slots_a:(g + 1) * slots_a, :] for g in range(na_g)], ngb, slots_a)
    out[1] = density(
        [gsum[m, g * capb:(g + 1) * capb, :] for m in range(nbo) for g in range(nb_g)], 0, capb)

    for group in (list(xcopies.values()), list(ocopies.values()), list(fcopies.values()),
                  list(acopies.values()), pcopies, rcopies):
        for c in group:
            c.wait_send()

    @pl.loop(1, everyone)
    def _(d):
        spread(d).wait_send()


def body(mesh, civec, acoup, asrc, apair, acnt, bcoup, bsrc, bpair, bcnt):
    na, nb, no = mesh.shape["alpha"], mesh.shape["beta"], mesh.shape["orb"]
    nbo = nb * no
    rows, cols = civec.shape
    ta, tb = acnt.shape[0], bcnt.shape[0]
    capa, capb = asrc.shape[0] // ta, bsrc.shape[0] // tb
    width = cols // na
    chunks = (rows // 2, rows // 2)
    ahead = len(chunks)
    nq, nc = len(chunks), width // LANES
    slots_a = 8
    groups, groups_a = bpair.shape[0] // LANES, ta * slots_a // LANES
    cfg = (na, nb, no, chunks, ahead, capa, capb, ta, tb, width, cols)
    anyspace = pl.BlockSpec(memory_space=pl.ANY)
    vmem = pl.BlockSpec(memory_space=pltpu.VMEM)
    dma = pltpu.SemaphoreType.DMA
    return pl.pallas_call(
        functools.partial(kernel, cfg),
        out_shape=jax.ShapeDtypeStruct((2, NPAIR // na, NPAIR // nbo), F32),
        in_specs=[anyspace] * 9,
        out_specs=vmem,
        scratch_shapes=[pltpu.VMEM((cols * nbo // LANES, n, LANES), BF16) for n in chunks] + [
            pltpu.VMEM((rows * na // LANES, LANES, LANES), BF16) for _ in range(nc)] + [
            pltpu.SMEM(x.shape, jnp.int32) for x in (asrc, apair, acnt, bsrc, bpair, bcnt)] + [
            pltpu.VMEM(acoup.shape, BF16),
            pltpu.VMEM(bcoup.shape, BF16),
            pltpu.VMEM((capb * ROWT, max(chunks) // ROWT * LANES), BF16),
            pltpu.VMEM((capb * ROWT, max(chunks) // ROWT * LANES), BF16),
            pltpu.VMEM((slots_a * ROWT, LANES // ROWT * LANES), BF16),
            pltpu.VMEM((slots_a * ROWT, LANES // ROWT * LANES), BF16),
            pltpu.VMEM((tb, capb, capb * ROWT), F32),
            pltpu.VMEM((ta, slots_a, slots_a * ROWT), F32),
            pltpu.VMEM((nbo, groups, LANES), jnp.int32),
            pltpu.VMEM((up(NPAIR // na, 16), (nbo * groups + groups_a) * LANES), BF16),
            pltpu.VMEM((nbo * groups + groups_a, LANES, up(NPAIR // nbo, LANES)), BF16),
            pltpu.VMEM((na, 8, LANES), F32),
            pltpu.VMEM((na, 8, LANES), F32),
            pltpu.VMEM((na, nbo, 8, LANES), F32),
            pltpu.VMEM((nbo + 1, groups * capb, LANES), F32),
            dma((8,)), dma((nc,)), dma((nq, cols // LANES)),
            dma((nq, nb)), dma((nq, nb)), dma((nq,)), dma((nq,)), dma((nq, nb)), dma((nq, nb)),
            dma((nc, na)), dma((nc, na)), dma((nbo,)), dma((nbo,)),
            dma((na,)), dma((na,)), dma((na * nbo,)), dma((na * nbo,)),
        ],
        compiler_params=pltpu.CompilerParams(
            collective_id=0, has_side_effects=True, vmem_limit_bytes=60 * 1024 * 1024),
    )(civec.reshape(-1, LANES, cols), acoup, asrc, apair, acnt, bcoup, bsrc, bpair, bcnt)


def solution(mesh):
    return jax.shard_map(
        functools.partial(body, mesh),
        mesh=mesh,
        in_specs=(
            P(("frag", "alpha"), ("beta", "orb")),
            P("frag", None, None),
            P("frag"),
            P("frag"),
            P("frag"),
            P(("frag", "beta", "orb"), None, None),
            P(("frag", "beta", "orb")),
            P(("frag", "beta", "orb")),
            P(("frag", "beta", "orb")),
        ),
        out_specs=P("frag", "alpha", ("beta", "orb")),
        check_vma=False,
    )
```
